32 devices in a mesh: grp: 2 (over x), ka: 16 (over z, y, core).
Axes of the slice: x: 2, y: 2, z: 4, core: 2. Of those that a mesh axis runs over, the one named last changes fastest.
Arguments:
- wannier_table: float32 [2, 2048, 8192], P(None, 'grp', 'ka'), parts along dimension 1, may hold values from -0.125 to 0.125
- lattice: int32 [3, 2048], P(None, 'grp'), parts along dimension 1, may hold values from -12 to 12
- kpoint_grid: int32 [3, 2048], P(None, ('grp', 'ka')), parts along dimension 1, may hold values from 0 to 63
- eigen_vectors: float32 [2048, 64, 128], P(('grp', 'ka')), parts along dimension 0, may hold values from -0.5 to 0.5
- target_owner: int32 [2048], P(('grp', 'ka')), parts along dimension 0, may hold values from 0 to 15, as said below
- target_slot: int32 [2048], P(('grp', 'ka')), parts along dimension 0, may hold values from 0 to 63
Outputs:
- rotated_coupling: float32 [2048, 2, 64, 128], P(('grp', 'ka')), parts along dimension 0
The draws below stay inside these ranges and needn't reach their ends.
There are 2 independent parts, one for each index of `grp`. The reference program is written for one: setup_inputs(seed, part) draws one part's arguments, and reference() takes and returns one part's arrays. A program takes and returns all parts, laid end to end along the dimension named above; each array names one. Nothing has to cross between parts.
Inputs may be any that keep to these rules, and one draw needn't show every extreme that they name: target_owner[k] * 64 + target_slot[k] over all k is a permutation of the 1024 k-points. The 64 k-points of one index of ka ask at most 8 of them of any one owner, and every device asks exactly 8 of some owner.
All inputs are finite; a program needn't handle non-finite values.
Results may differ from the reference program's by a relative error of at most 0.0003.
Values sent between devices are 32-bit elements; how exact they have to be, the bound alone decides.
A program may use at most 128 MiB of HBM per device.

```python
import math
import jax
import jax.numpy as jnp
from jax import lax

NW = 64
NMODE = 2
NRVEC = 1024
KMESH = 64
K_DEV = 64
KPTS = 1024
PAIRS = 8192
N_KA = 16


def target_pairs(key):
    base = jax.random.fold_in(key, 17)
    key_pairing, key_excess, key_offsets, key_slots, key_order = jax.random.split(base, 5)
    per_owner = K_DEV // N_KA
    halves = N_KA // 2
    pairing = jax.random.permutation(key_pairing, N_KA)
    excess = jax.random.randint(key_excess, (halves,), 0, per_owner + 1).astype(jnp.int32).at[0].set(per_owner)
    multiplicity = jnp.zeros((N_KA,), jnp.int32).at[pairing[:halves]].set(per_owner + excess).at[pairing[halves:]].set(per_owner - excess)
    offsets = jnp.repeat(jnp.arange(N_KA, dtype=jnp.int32), multiplicity, total_repeat_length=K_DEV)
    offsets = jax.random.permutation(key_offsets, offsets)
    slots = jax.random.permutation(key_slots, K_DEV).astype(jnp.int32)
    shuffles = jax.vmap(lambda subkey: jax.random.permutation(subkey, K_DEV))(jax.random.split(key_order, N_KA))
    device_ids = jnp.arange(N_KA, dtype=jnp.int32)[:, None]
    owners = (device_ids + offsets[shuffles]) % N_KA
    local_slots = slots[shuffles]
    return (owners.reshape(-1).astype(jnp.int32), local_slots.reshape(-1).astype(jnp.int32))


def draw_target_owner(key, part):
    return target_pairs(key)[0]


def draw_target_slot(key, part):
    return target_pairs(key)[1]


def with_ends(drawn, key, smallest, high):
    shape = drawn.shape
    spot = [jax.random.randint(jax.random.fold_in(key, axis), (), 0, shape[axis]) for axis in range(len(shape))]
    drawn = drawn.at[tuple(spot)].set(smallest)
    longest = shape.index(max(shape))
    spot[longest] = (spot[longest] + 1) % shape[longest]
    return drawn.at[tuple(spot)].set(high)


def levels(rng, shape, shards, low, top_value):
    level = 1.0
    for axis_at, shards_of in shards:
        steps = jax.random.uniform(jax.random.fold_in(jax.random.fold_in(rng, 6), axis_at), (shards_of,), jnp.float32, low / len(shards), top_value / len(shards))
        level = level * jnp.repeat(jnp.exp(steps), shape[axis_at] // shards_of).reshape((-1,) + (1,) * (len(shape) - 1 - axis_at))
    return level


def scatter_about(key, extent, scale, most, cuts=(), kind=jnp.bfloat16):
    values = jax.random.normal(key, extent, jnp.float32) * scale
    if len(cuts) > 0:
        values = levels(key, extent, cuts, -0.22, 0.18) * values
    return jnp.clip(values, min=-most, max=most).astype(kind)


def setup_inputs(seed: int = 0, part: int = 0) -> dict:
    splits = jax.random.split(jax.random.key(seed), 7)
    own_keys = jax.random.split(jax.random.fold_in(splits[6], part), 7)
    wannier_table = scatter_about(own_keys[0], (2, NRVEC, PAIRS), (2 * NRVEC) ** -0.5, 0.125, ((2, 16),), jnp.float32)
    lattice = with_ends(jax.random.randint(own_keys[1], (3, NRVEC), -12, 13), jax.random.fold_in(own_keys[1], 1), -12, 12).astype(jnp.int32)
    kpoint_grid = with_ends(jax.random.randint(own_keys[2], (3, KPTS), 0, KMESH), jax.random.fold_in(own_keys[2], 1), 0, KMESH - 1).astype(jnp.int32)
    eigen_vectors = scatter_about(own_keys[3], (KPTS, NW, 2 * NW), (2 * NW) ** -0.5, 0.5, ((0, 16),), jnp.float32)
    target_owner = draw_target_owner(jax.random.fold_in(jax.random.fold_in(splits[6], part), 71), part)
    target_slot = draw_target_slot(jax.random.fold_in(jax.random.fold_in(splits[6], part), 71), part)
    return {"wannier_table": wannier_table, "lattice": lattice, "kpoint_grid": kpoint_grid, "eigen_vectors": eigen_vectors, "target_owner": target_owner, "target_slot": target_slot}


def phases(grid_block, lattice):
    products = grid_block[0][:, None] * lattice[0][None, :] + grid_block[1][:, None] * lattice[1][None, :] + grid_block[2][:, None] * lattice[2][None, :]
    angles = jnp.mod(products, KMESH).astype(jnp.float32) * (2.0 * math.pi / KMESH)
    return jnp.cos(angles), jnp.sin(angles)


def rotate(real_part, imag_part, near_vectors, far_vectors):
    orbitals = near_vectors.shape[1]
    highest = lax.Precision.HIGHEST
    near_swap = jnp.concatenate([-near_vectors[..., orbitals:], near_vectors[..., :orbitals]], -1)
    right_done = jnp.einsum("kamn,knj->kamj", real_part, near_vectors, precision=highest) + jnp.einsum("kamn,knj->kamj", imag_part, near_swap, precision=highest)
    right_swap = jnp.concatenate([right_done[..., orbitals:], -right_done[..., :orbitals]], -1)
    return jnp.einsum("kmi,kamj->kaij", far_vectors[..., :orbitals], right_done, precision=highest) + jnp.einsum("kmi,kamj->kaij", far_vectors[..., orbitals:], right_swap, precision=highest)


def reference(wannier_table, lattice, kpoint_grid, eigen_vectors, target_owner, target_slot):
    block_rows = math.gcd(KPTS, 512)
    highest = lax.Precision.HIGHEST
    target = (target_owner * K_DEV + target_slot).astype(jnp.int32)

    def one_block(block_id):
        first = (block_id * block_rows).astype(jnp.int32)
        grid_block = lax.dynamic_slice_in_dim(kpoint_grid, first, block_rows, 1)
        cosine, sine_part = phases(grid_block, lattice)
        real_part = jnp.dot(cosine, wannier_table[0], precision=highest) - jnp.dot(sine_part, wannier_table[1], precision=highest)
        imag_part = jnp.dot(cosine, wannier_table[1], precision=highest) + jnp.dot(sine_part, wannier_table[0], precision=highest)
        real_part = real_part.reshape(block_rows, NMODE, NW, NW)
        imag_part = imag_part.reshape(block_rows, NMODE, NW, NW)
        near_vectors = lax.dynamic_slice_in_dim(eigen_vectors, first, block_rows, 0)
        far_vectors = eigen_vectors[lax.dynamic_slice_in_dim(target, first, block_rows, 0)]
        return rotate(real_part, imag_part, near_vectors, far_vectors)

    blocks = lax.map(one_block, jnp.arange(KPTS // block_rows, dtype=jnp.int32))
    return blocks.reshape(KPTS, NMODE, NW, 2 * NW)
```

```python
import functools
import math

import jax
import jax.numpy as jnp
from jax import lax
from jax.experimental import pallas as pl
from jax.experimental.pallas import tpu as pltpu
from jax.sharding import PartitionSpec as P

KMESH = 64
MESH = pl.DeviceIdType.MESH


def phase_matrix(grid_block, lattice):
    products = (
        grid_block[0][:, None] * lattice[0][None, :]
        + grid_block[1][:, None] * lattice[1][None, :]
        + grid_block[2][:, None] * lattice[2][None, :]
    )
    angles = jnp.mod(products, KMESH).astype(jnp.float32) * (2.0 * math.pi / KMESH)
    cosine = jnp.cos(angles)
    sine_part = jnp.sin(angles)
    upper_rows = jnp.concatenate([cosine, -sine_part], 1)
    lower_rows = jnp.concatenate([sine_part, cosine], 1)
    return jnp.concatenate([upper_rows, lower_rows], 0)


def rotate(real_part, imag_part, near_vectors, far_vectors):
    orbitals = near_vectors.shape[1]
    highest = lax.Precision.HIGHEST
    near_swap = jnp.concatenate([-near_vectors[..., orbitals:], near_vectors[..., :orbitals]], -1)
    right_done = jnp.einsum(
        "kamn,knj->kamj", real_part, near_vectors, precision=highest
    ) + jnp.einsum("kamn,knj->kamj", imag_part, near_swap, precision=highest)
    right_swap = jnp.concatenate([right_done[..., orbitals:], -right_done[..., :orbitals]], -1)
    return jnp.einsum(
        "kmi,kamj->kaij", far_vectors[..., :orbitals], right_done, precision=highest
    ) + jnp.einsum("kmi,kamj->kaij", far_vectors[..., orbitals:], right_swap, precision=highest)


def fetch_far(eigen_vectors, target_owner, target_slot, devices):
    kpoints = eigen_vectors.shape[0]
    orbitals = eigen_vectors.shape[1]
    capacity = 2 * kpoints // devices
    owners_onehot = (target_owner[:, None] == jnp.arange(devices, dtype=jnp.int32)[None, :]).astype(
        jnp.int32
    )
    before = jnp.cumsum(owners_onehot, 0) - owners_onehot
    position = jnp.sum(before * owners_onehot, 1)
    flat_index = target_owner * capacity + position
    wanted = (
        jnp.zeros((devices * capacity,), jnp.int32)
        .at[flat_index]
        .set(target_slot)
        .reshape(devices, capacity)
    )
    picked = eigen_vectors[lax.all_to_all(wanted, "ka", split_axis=0, concat_axis=0, tiled=True)]
    fetched = lax.all_to_all(picked, "ka", split_axis=0, concat_axis=0, tiled=True)
    return fetched.reshape(devices * capacity, orbitals, 2 * orbitals)[flat_index]


def interpolate(wannier_table, lattice, kpoint_grid, kpoints, devices):
    vectors = wannier_table.shape[1]
    local_pairs = wannier_table.shape[2]
    highest = lax.Precision.HIGHEST
    grid_all = lax.all_gather(kpoint_grid, "ka", axis=1, tiled=True)
    per_block = 1
    while (
        per_block * 2 <= devices
        and devices % (per_block * 2) == 0
        and (per_block * 2 * kpoints <= 512)
    ):
        per_block = per_block * 2
    block_rows = per_block * kpoints
    flat_table = wannier_table.reshape(2 * vectors, local_pairs)

    def fill_block(block_id, collected):
        grid_block = lax.dynamic_slice_in_dim(grid_all, block_id * block_rows, block_rows, 1)
        result = jnp.dot(
            phase_matrix(grid_block, lattice),
            flat_table,
            precision=highest,
            preferred_element_type=jnp.float32,
        )
        return lax.dynamic_update_slice_in_dim(
            collected, result.reshape(2, block_rows, local_pairs), block_id * block_rows, 1
        )

    initial = jnp.zeros((2, kpoints * devices, local_pairs), jnp.float32)
    computed = lax.fori_loop(0, devices // per_block, fill_block, initial)
    return lax.all_to_all(computed, "ka", split_axis=1, concat_axis=2, tiled=True)


def local(wannier_table, lattice, kpoint_grid, eigen_vectors, target_owner, target_slot):
    kpoints = eigen_vectors.shape[0]
    orbitals = eigen_vectors.shape[1]
    devices = lax.axis_size("ka")
    interpolated = interpolate(wannier_table, lattice, kpoint_grid, kpoints, devices)
    far_vectors = fetch_far(eigen_vectors, target_owner, target_slot, devices)
    real_part = interpolated[0].reshape(kpoints, -1, orbitals, orbitals)
    imag_part = interpolated[1].reshape(kpoints, -1, orbitals, orbitals)
    return rotate(real_part, imag_part, eigen_vectors, far_vectors)


def cos_sin(index):
    quarter = KMESH // 4
    shifted = index + quarter // 2
    quadrant = shifted // quarter if quarter & (quarter - 1) else shifted >> (quarter.bit_length() - 1)
    arc = (index - quadrant * quarter).astype(jnp.float32) * (2.0 * math.pi / KMESH)
    square = arc * arc
    sine = arc * (
        1.0 + square * (-1.0 / 6 + square * (1.0 / 120 + square * (-1.0 / 5040 + square * (1.0 / 362880))))
    )
    cosine = 1.0 + square * (
        -0.5
        + square
        * (1.0 / 24 + square * (-1.0 / 720 + square * (1.0 / 40320 + square * (-1.0 / 3628800))))
    )
    swapped = (quadrant & 1) == 1
    out_cos = jnp.where(swapped, sine, cosine)
    out_sin = jnp.where(swapped, cosine, sine)
    out_cos = jnp.where(((quadrant + 1) & 2) == 2, -out_cos, out_cos)
    out_sin = jnp.where((quadrant & 2) == 2, -out_sin, out_sin)
    return out_cos, out_sin


def split(value):
    high = value.astype(jnp.bfloat16)
    return high, (value - high.astype(jnp.float32)).astype(jnp.bfloat16)


def dot(left, right):
    return jnp.dot(left, right, preferred_element_type=jnp.float32)


def kernel(
    sizes,
    table_hbm,
    eigen_hbm,
    letters,
    lattice,
    flat_index,
    out_hbm,
    table,
    eigen,
    table_high,
    table_low,
    inbox,
    inbox_scalar,
    far_out,
    far_in,
    entries_out,
    entries_in,
    waves,
    near_parts,
    far_parts,
    result,
    load_sem,
    scalar_sem,
    letter_send,
    letter_recv,
    far_send,
    far_recv,
    entry_send,
    entry_recv,
    store_sem,
):
    n, kpoints, orbitals, vectors, pairs, capacity, per_group, chunks = sizes
    rows = pairs // orbitals
    wide = 2 * orbitals
    modes = n * rows // orbitals
    per_chunk = kpoints // chunks
    me = lax.axis_index("ka")

    load_table = pltpu.make_async_copy(table_hbm, table, load_sem.at[0])
    load_eigen = pltpu.make_async_copy(eigen_hbm, eigen, load_sem.at[1])
    load_eigen.start()
    load_table.start()

    barrier = pltpu.get_barrier_semaphore()

    @pl.loop(1, n)
    def _(step):
        other = lax.rem(me + step, n)
        pl.semaphore_signal(barrier, inc=1, device_id={"ka": other}, device_id_type=MESH)

    pl.semaphore_wait(barrier, n - 1)

    def send_letter(step):
        other = lax.rem(me + step, n)
        return pltpu.make_async_remote_copy(
            src_ref=letters.at[other],
            dst_ref=inbox.at[me],
            send_sem=letter_send.at[other],
            recv_sem=letter_recv.at[me],
            device_id={"ka": other},
            device_id_type=MESH,
        )

    def recv_letter(step):
        other = lax.rem(me + step, n)
        return pltpu.make_async_remote_copy(
            src_ref=letters.at[other],
            dst_ref=inbox.at[other],
            send_sem=letter_send.at[other],
            recv_sem=letter_recv.at[other],
            device_id={"ka": other},
            device_id_type=MESH,
        )

    def send_far(step):
        other = lax.rem(me + step, n)
        return pltpu.make_async_remote_copy(
            src_ref=far_out.at[other],
            dst_ref=far_in.at[me],
            send_sem=far_send.at[other],
            recv_sem=far_recv.at[me],
            device_id={"ka": other},
            device_id_type=MESH,
        )

    def recv_far(step):
        other = lax.rem(me + step, n)
        return pltpu.make_async_remote_copy(
            src_ref=far_out.at[other],
            dst_ref=far_in.at[other],
            send_sem=far_send.at[other],
            recv_sem=far_recv.at[other],
            device_id={"ka": other},
            device_id_type=MESH,
        )

    def entries(step, chunk, receive):
        other = lax.rem(me + step, n)
        part = pl.ds(chunk * per_chunk * rows, per_chunk * rows)
        slot = other if receive else me
        return pltpu.make_async_remote_copy(
            src_ref=entries_out.at[other, part],
            dst_ref=entries_in.at[slot, part],
            send_sem=entry_send.at[other, chunk],
            recv_sem=entry_recv.at[slot, chunk],
            device_id={"ka": other},
            device_id_type=MESH,
        )

    @pl.loop(1, n)
    def _(step):
        send_letter(step).start()

    inbox[me] = letters[me]

    @pl.loop(1, n)
    def _(step):
        recv_letter(step).wait_recv()

    to_scalar = pltpu.make_async_copy(inbox, inbox_scalar, scalar_sem.at[0])
    to_scalar.start()
    to_scalar.wait()
    load_eigen.wait()

    def far_order(step):
        return lax.rem(step + n // 2, n)

    @pl.loop(0, n)
    def _(step):
        offset = far_order(step)
        other = lax.rem(me + offset, n)
        for slot in range(capacity):
            far_out[other, slot] = eigen[inbox_scalar[other, 3, slot]]

        @pl.when(offset != 0)
        def _():
            send_far(offset).start()

    own_far = pltpu.make_async_copy(far_out.at[me], far_in.at[me], scalar_sem.at[1])
    own_far.start()

    load_table.wait()
    piece = 128

    @pl.loop(0, vectors // piece)
    def _(step):
        part = pl.ds(pl.multiple_of(step * piece, piece), piece)
        for which in range(2):
            high, low = split(table[which, part, :])
            table_high[which, part, :] = high
            table_low[which, part, :] = low

    group_rows = per_group * kpoints
    lanes = lax.broadcasted_iota(jnp.int32, (group_rows, wide), 1)
    first_half = lanes < orbitals

    @pl.loop(0, n // per_group)
    def _(group):
        for local_at in range(per_group):
            other = lax.rem(me + far_order(group * per_group + local_at), n)
            turned = inbox[other].T
            coords = [turned[:kpoints, axis : axis + 1] for axis in range(3)]

            @pl.loop(0, vectors // piece)
            def _(step):
                part = pl.ds(pl.multiple_of(step * piece, piece), piece)
                products = (
                    coords[0] * lattice[0:1, part]
                    + coords[1] * lattice[1:2, part]
                    + coords[2] * lattice[2:3, part]
                )
                cosine, sine = cos_sin(products & (KMESH - 1))
                own_rows = pl.ds(local_at * kpoints, kpoints)
                cos_high, cos_low = split(cosine)
                sin_high, sin_low = split(sine)
                waves[0, own_rows, part] = cos_high
                waves[1, own_rows, part] = cos_low
                waves[2, own_rows, part] = sin_high
                waves[3, own_rows, part] = sin_low

        block = min(256, pairs)
        for first in range(0, pairs, block):
            cols = slice(first, first + block)

            def product(wave, which):
                return (
                    dot(waves[wave], table_high[which, :, cols])
                    + dot(waves[wave], table_low[which, :, cols])
                    + dot(waves[wave + 1], table_high[which, :, cols])
                )

            real = product(0, 0) - product(2, 1)
            imag = product(0, 1) + product(2, 0)
            for pair in range(block // wide):
                span = slice(pair * wide, (pair + 1) * wide)
                real_part, imag_part = real[:, span], imag[:, span]
                even = jnp.where(first_half, real_part, pltpu.roll(imag_part, orbitals, 1))
                odd = jnp.where(first_half, pltpu.roll(real_part, orbitals, 1), imag_part)
                row = first // orbitals + 2 * pair
                for local_at in range(per_group):
                    other = lax.rem(me + far_order(group * per_group + local_at), n)
                    own = slice(local_at * kpoints, (local_at + 1) * kpoints)
                    entries_out[other, pl.ds(row, kpoints, stride=rows), :] = even[own]
                    entries_out[other, pl.ds(row + 1, kpoints, stride=rows), :] = odd[own]

    for chunk in range(chunks):

        @pl.loop(0, n)
        def _(step):
            offset = far_order(step)

            @pl.when(offset != 0)
            def _():
                entries(offset, chunk, False).start()

    own_entries = pltpu.make_async_copy(entries_out.at[me], entries_in.at[me], scalar_sem.at[2])
    own_entries.start()

    half_lane = lax.broadcasted_iota(jnp.int32, (orbitals, wide), 1) < orbitals

    @pl.loop(0, kpoints)
    def _(k):
        near = eigen[k]
        turned = pltpu.roll(near, orbitals, 1)
        lower = jnp.where(half_lane, -turned, turned)
        high, low = split(jnp.concatenate([near, lower], 0))
        near_parts[k] = jnp.concatenate([high, low], 1)

    own_far.wait()

    @pl.loop(1, n)
    def _(step):
        recv_far(step).wait_recv()

    @pl.loop(0, kpoints)
    def _(k):
        at = flat_index[k]
        far = far_in[at // capacity, lax.rem(at, capacity)]
        high = far.astype(jnp.bfloat16).astype(jnp.float32)
        far_parts[k] = jnp.concatenate([high, far - high], 0).T.astype(jnp.bfloat16)

    own_entries.wait()

    def rotate_one(k):
        matrix = entries_in[:, pl.ds(pl.multiple_of(k * rows, rows), rows), :].reshape(n * rows, wide)
        high, low = split(matrix)
        near = near_parts[k]
        right = dot(jnp.concatenate([high, low], 1), jnp.concatenate([near, near], 0))
        right = right[:, :wide] + right[:, wide:]
        right = jnp.concatenate(
            [right[mode * orbitals : (mode + 1) * orbitals] for mode in range(modes)], 1
        )
        high, low = split(right)
        far = far_parts[k]
        both = dot(jnp.concatenate([far, far], 1), jnp.concatenate([high, high, low, low], 0))
        for mode in range(modes):
            span = both[:, mode * wide : (mode + 1) * wide]
            turned = pltpu.roll(span[orbitals:], orbitals, 1)
            result[k, mode] = span[:orbitals] + jnp.where(half_lane, turned, -turned)

    def store(chunk):
        part = pl.ds(chunk * per_chunk, per_chunk)
        return pltpu.make_async_copy(result.at[part], out_hbm.at[part], store_sem.at[chunk])

    together = 2 if per_chunk % 2 == 0 else 1
    for chunk in range(chunks):

        @pl.loop(1, n)
        def _(step):
            entries(step, chunk, True).wait_recv()

        @pl.loop(0, per_chunk // together)
        def _(step):
            for extra in range(together):
                rotate_one(chunk * per_chunk + step * together + extra)

        store(chunk).start()

    for chunk in range(chunks):
        store(chunk).wait()

        @pl.loop(1, n)
        def _(step):
            entries(step, chunk, False).wait_send()

    @pl.loop(1, n)
    def _(step):
        send_letter(step).wait_send()
        send_far(step).wait_send()


def fused(wannier_table, lattice, kpoint_grid, eigen_vectors, target_owner, target_slot):
    n = lax.axis_size("ka")
    kpoints, orbitals, wide = eigen_vectors.shape
    vectors, pairs = wannier_table.shape[1:]
    capacity = 2 * kpoints // n
    rows = pairs // orbitals
    modes = n * rows // orbitals
    per_group = math.gcd(n, 4)
    chunks = math.gcd(kpoints, 4)

    ids = jnp.arange(kpoints, dtype=jnp.int32)
    same = (target_owner[:, None] == target_owner[None, :]) & (ids[None, :] < ids[:, None])
    position = jnp.sum(same.astype(jnp.int32), 1)
    flat_index = target_owner * capacity + position
    places = jnp.arange(n * capacity, dtype=jnp.int32)
    wanted = jnp.sum(
        jnp.where(places[:, None] == flat_index[None, :], target_slot[None, :], 0), 1
    ).reshape(n, 1, capacity)
    wanted = jnp.pad(wanted, ((0, 0), (3, 4), (0, 128 - capacity)))
    letters = wanted + jnp.pad(kpoint_grid, ((0, 5), (0, 128 - kpoints)))[None]

    f32, bf16 = jnp.float32, jnp.bfloat16
    sizes = (n, kpoints, orbitals, vectors, pairs, capacity, per_group, chunks)
    return pl.pallas_call(
        functools.partial(kernel, sizes),
        out_shape=jax.ShapeDtypeStruct((kpoints, modes, orbitals, wide), f32),
        in_specs=[
            pl.BlockSpec(memory_space=pl.ANY),
            pl.BlockSpec(memory_space=pl.ANY),
            pl.BlockSpec(memory_space=pltpu.VMEM),
            pl.BlockSpec(memory_space=pltpu.VMEM),
            pl.BlockSpec(memory_space=pltpu.SMEM),
        ],
        out_specs=pl.BlockSpec(memory_space=pl.ANY),
        scratch_shapes=[
            pltpu.VMEM((2, vectors, pairs), f32),
            pltpu.VMEM((kpoints, orbitals, wide), f32),
            pltpu.VMEM((2, vectors, pairs), bf16),
            pltpu.VMEM((2, vectors, pairs), bf16),
            pltpu.VMEM((n, 8, 128), jnp.int32),
            pltpu.SMEM((n, 8, 128), jnp.int32),
            pltpu.VMEM((n, capacity, orbitals, wide), f32),
            pltpu.VMEM((n, capacity, orbitals, wide), f32),
            pltpu.VMEM((n, kpoints * rows, wide), f32),
            pltpu.VMEM((n, kpoints * rows, wide), f32),
            pltpu.VMEM((4, per_group * kpoints, vectors), bf16),
            pltpu.VMEM((kpoints, wide, 2 * wide), bf16),
            pltpu.VMEM((kpoints, wide, wide), bf16),
            pltpu.VMEM((kpoints, modes, orbitals, wide), f32),
            pltpu.SemaphoreType.DMA((2,)),
            pltpu.SemaphoreType.DMA((3,)),
            pltpu.SemaphoreType.DMA((n,)),
            pltpu.SemaphoreType.DMA((n,)),
            pltpu.SemaphoreType.DMA((n,)),
            pltpu.SemaphoreType.DMA((n,)),
            pltpu.SemaphoreType.DMA((n, chunks)),
            pltpu.SemaphoreType.DMA((n, chunks)),
            pltpu.SemaphoreType.DMA((chunks,)),
        ],
        compiler_params=pltpu.CompilerParams(
            collective_id=0, has_side_effects=True, vmem_limit_bytes=60 * 1024 * 1024
        ),
    )(wannier_table, eigen_vectors, letters, lattice, flat_index)


def part(wannier_table, lattice, kpoint_grid, eigen_vectors, target_owner, target_slot):
    rows = wannier_table.shape[2] // eigen_vectors.shape[1]
    tiled = rows % 8 == 0 and wannier_table.shape[1] % 128 == 0 and eigen_vectors.shape[2] == 128
    step = fused if tiled else local
    return step(wannier_table, lattice, kpoint_grid, eigen_vectors, target_owner, target_slot)


def solution(mesh):
    placed = (
        P(None, "grp", "ka"),
        P(None, "grp"),
        P(None, ("grp", "ka")),
        P(("grp", "ka"), None, None),
        P(("grp", "ka")),
        P(("grp", "ka")),
    )
    return jax.shard_map(
        part,
        mesh=mesh,
        in_specs=placed,
        out_specs=P(("grp", "ka"), None, None, None),
        check_vma=False,
    )
```

```python
import functools
import math

import jax
import jax.numpy as jnp
from jax import lax
from jax.experimental import pallas as pl
from jax.experimental.pallas import tpu as pltpu
from jax.sharding import PartitionSpec as P

KMESH = 64
MESH = pl.DeviceIdType.MESH


def phase_matrix(grid_block, lattice):
    products = (
        grid_block[0][:, None] * lattice[0][None, :]
        + grid_block[1][:, None] * lattice[1][None, :]
        + grid_block[2][:, None] * lattice[2][None, :]
    )
    angles = jnp.mod(products, KMESH).astype(jnp.float32) * (2.0 * math.pi / KMESH)
    cosine = jnp.cos(angles)
    sine_part = jnp.sin(angles)
    upper_rows = jnp.concatenate([cosine, -sine_part], 1)
    lower_rows = jnp.concatenate([sine_part, cosine], 1)
    return jnp.concatenate([upper_rows, lower_rows], 0)


def rotate(real_part, imag_part, near_vectors, far_vectors):
    orbitals = near_vectors.shape[1]
    highest = lax.Precision.HIGHEST
    near_swap = jnp.concatenate([-near_vectors[..., orbitals:], near_vectors[..., :orbitals]], -1)
    right_done = jnp.einsum(
        "kamn,knj->kamj", real_part, near_vectors, precision=highest
    ) + jnp.einsum("kamn,knj->kamj", imag_part, near_swap, precision=highest)
    right_swap = jnp.concatenate([right_done[..., orbitals:], -right_done[..., :orbitals]], -1)
    return jnp.einsum(
        "kmi,kamj->kaij", far_vectors[..., :orbitals], right_done, precision=highest
    ) + jnp.einsum("kmi,kamj->kaij", far_vectors[..., orbitals:], right_swap, precision=highest)


def fetch_far(eigen_vectors, target_owner, target_slot, devices):
    kpoints = eigen_vectors.shape[0]
    orbitals = eigen_vectors.shape[1]
    capacity = 2 * kpoints // devices
    owners_onehot = (target_owner[:, None] == jnp.arange(devices, dtype=jnp.int32)[None, :]).astype(
        jnp.int32
    )
    before = jnp.cumsum(owners_onehot, 0) - owners_onehot
    position = jnp.sum(before * owners_onehot, 1)
    flat_index = target_owner * capacity + position
    wanted = (
        jnp.zeros((devices * capacity,), jnp.int32)
        .at[flat_index]
        .set(target_slot)
        .reshape(devices, capacity)
    )
    picked = eigen_vectors[lax.all_to_all(wanted, "ka", split_axis=0, concat_axis=0, tiled=True)]
    fetched = lax.all_to_all(picked, "ka", split_axis=0, concat_axis=0, tiled=True)
    return fetched.reshape(devices * capacity, orbitals, 2 * orbitals)[flat_index]


def interpolate(wannier_table, lattice, kpoint_grid, kpoints, devices):
    vectors = wannier_table.shape[1]
    local_pairs = wannier_table.shape[2]
    highest = lax.Precision.HIGHEST
    grid_all = lax.all_gather(kpoint_grid, "ka", axis=1, tiled=True)
    per_block = 1
    while (
        per_block * 2 <= devices
        and devices % (per_block * 2) == 0
        and (per_block * 2 * kpoints <= 512)
    ):
        per_block = per_block * 2
    block_rows = per_block * kpoints
    flat_table = wannier_table.reshape(2 * vectors, local_pairs)

    def fill_block(block_id, collected):
        grid_block = lax.dynamic_slice_in_dim(grid_all, block_id * block_rows, block_rows, 1)
        result = jnp.dot(
            phase_matrix(grid_block, lattice),
            flat_table,
            precision=highest,
            preferred_element_type=jnp.float32,
        )
        return lax.dynamic_update_slice_in_dim(
            collected, result.reshape(2, block_rows, local_pairs), block_id * block_rows, 1
        )

    initial = jnp.zeros((2, kpoints * devices, local_pairs), jnp.float32)
    computed = lax.fori_loop(0, devices // per_block, fill_block, initial)
    return lax.all_to_all(computed, "ka", split_axis=1, concat_axis=2, tiled=True)


def local(wannier_table, lattice, kpoint_grid, eigen_vectors, target_owner, target_slot):
    kpoints = eigen_vectors.shape[0]
    orbitals = eigen_vectors.shape[1]
    devices = lax.axis_size("ka")
    interpolated = interpolate(wannier_table, lattice, kpoint_grid, kpoints, devices)
    far_vectors = fetch_far(eigen_vectors, target_owner, target_slot, devices)
    real_part = interpolated[0].reshape(kpoints, -1, orbitals, orbitals)
    imag_part = interpolated[1].reshape(kpoints, -1, orbitals, orbitals)
    return rotate(real_part, imag_part, eigen_vectors, far_vectors)


def cos_sin(index):
    quarter = KMESH // 4
    shifted = index + quarter // 2
    quadrant = shifted // quarter if quarter & (quarter - 1) else shifted >> (quarter.bit_length() - 1)
    arc = (index - quadrant * quarter).astype(jnp.float32) * (2.0 * math.pi / KMESH)
    square = arc * arc
    sine = arc * (
        1.0 + square * (-1.0 / 6 + square * (1.0 / 120 + square * (-1.0 / 5040 + square * (1.0 / 362880))))
    )
    cosine = 1.0 + square * (
        -0.5
        + square
        * (1.0 / 24 + square * (-1.0 / 720 + square * (1.0 / 40320 + square * (-1.0 / 3628800))))
    )
    swapped = (quadrant & 1) == 1
    out_cos = jnp.where(swapped, sine, cosine)
    out_sin = jnp.where(swapped, cosine, sine)
    out_cos = jnp.where(((quadrant + 1) & 2) == 2, -out_cos, out_cos)
    out_sin = jnp.where((quadrant & 2) == 2, -out_sin, out_sin)
    return out_cos, out_sin


def split(value):
    high = value.astype(jnp.bfloat16)
    return high, (value - high.astype(jnp.float32)).astype(jnp.bfloat16)


def dot(left, right):
    return jnp.dot(left, right, preferred_element_type=jnp.float32)


def kernel(
    sizes,
    table_hbm,
    eigen_hbm,
    grid_own,
    lattice,
    owner_row,
    slot_row,
    out_hbm,
    table,
    eigen,
    table_high,
    table_low,
    letter,
    inbox,
    inbox_scalar,
    far_out,
    far_in,
    entries_out,
    entries_in,
    waves,
    near_parts,
    far_parts,
    result,
    load_sem,
    scalar_sem,
    letter_send,
    letter_recv,
    far_send,
    far_recv,
    entry_send,
    entry_recv,
    store_sem,
):
    n, kpoints, orbitals, vectors, pairs, capacity, per_group, chunks = sizes
    rows = pairs // orbitals
    wide = 2 * orbitals
    modes = n * rows // orbitals
    starts = [sum(chunks[:at]) for at in range(len(chunks))]
    me = lax.axis_index("ka")

    load_table = pltpu.make_async_copy(table_hbm, table, load_sem.at[0])
    load_eigen = pltpu.make_async_copy(eigen_hbm, eigen, load_sem.at[1])
    load_eigen.start()
    load_table.start()

    square = (128, 128)
    owners = jnp.broadcast_to(
        jnp.concatenate([owner_row[...], jnp.full((1, 128 - kpoints), n, jnp.int32)], 1), square
    )
    slots = jnp.broadcast_to(
        jnp.concatenate([slot_row[...], jnp.zeros((1, 128 - kpoints), jnp.int32)], 1), square
    )
    owners_down, slots_down = owners.T, slots.T
    lane = lax.broadcasted_iota(jnp.int32, square, 1)
    down = lax.broadcasted_iota(jnp.int32, square, 0)
    same = owners == owners_down
    before = jnp.sum(jnp.where(same & (down < lane), 1, 0), 0, keepdims=True)
    before_down = jnp.sum(jnp.where(same & (lane < down), 1, 0), 1, keepdims=True)
    flat_row = owners[:1] * capacity + before
    flat_down = owners_down * capacity + before_down
    hit = (flat_down == lane) & (down < kpoints)
    wanted = jnp.sum(jnp.where(hit, slots_down, 0), 0, keepdims=True)
    letter[...] = jnp.zeros((8, 128), jnp.int32)
    letter[0:3, 0:kpoints] = grid_own[...]
    letter[3:4, :] = wanted
    letter[4:5, :] = flat_row

    barrier = pltpu.get_barrier_semaphore()

    @pl.loop(1, n)
    def _(step):
        other = lax.rem(me + step, n)
        pl.semaphore_signal(barrier, inc=1, device_id={"ka": other}, device_id_type=MESH)

    pl.semaphore_wait(barrier, n - 1)

    def send_letter(step):
        other = lax.rem(me + step, n)
        return pltpu.make_async_remote_copy(
            src_ref=letter,
            dst_ref=inbox.at[me],
            send_sem=letter_send.at[other],
            recv_sem=letter_recv.at[me],
            device_id={"ka": other},
            device_id_type=MESH,
        )

    def recv_letter(step):
        other = lax.rem(me + step, n)
        return pltpu.make_async_remote_copy(
            src_ref=letter,
            dst_ref=inbox.at[other],
            send_sem=letter_send.at[other],
            recv_sem=letter_recv.at[other],
            device_id={"ka": other},
            device_id_type=MESH,
        )

    def send_far(step):
        other = lax.rem(me + step, n)
        return pltpu.make_async_remote_copy(
            src_ref=far_out.at[other],
            dst_ref=far_in.at[me],
            send_sem=far_send.at[other],
            recv_sem=far_recv.at[me],
            device_id={"ka": other},
            device_id_type=MESH,
        )

    def recv_far(step):
        other = lax.rem(me + step, n)
        return pltpu.make_async_remote_copy(
            src_ref=far_out.at[other],
            dst_ref=far_in.at[other],
            send_sem=far_send.at[other],
            recv_sem=far_recv.at[other],
            device_id={"ka": other},
            device_id_type=MESH,
        )

    def entries(step, chunk, receive):
        other = lax.rem(me + step, n)
        part = pl.ds(starts[chunk] * rows, chunks[chunk] * rows)
        slot = other if receive else me
        return pltpu.make_async_remote_copy(
            src_ref=entries_out.at[other, part],
            dst_ref=entries_in.at[slot, part],
            send_sem=entry_send.at[other, chunk],
            recv_sem=entry_recv.at[slot, chunk],
            device_id={"ka": other},
            device_id_type=MESH,
        )

    @pl.loop(1, n)
    def _(step):
        send_letter(step).start()

    inbox[me] = letter[...]

    @pl.loop(1, n)
    def _(step):
        recv_letter(step).wait_recv()

    to_scalar = pltpu.make_async_copy(inbox, inbox_scalar, scalar_sem.at[0])
    to_scalar.start()
    to_scalar.wait()
    load_eigen.wait()

    @pl.loop(0, n)
    def _(step):
        other = lax.rem(me + step, n)
        for slot in range(capacity):
            far_out[other, slot] = eigen[inbox_scalar[other, 3, me * capacity + slot]]

        @pl.when(step != 0)
        def _():
            send_far(step).start()

    own_far = pltpu.make_async_copy(far_out.at[me], far_in.at[me], scalar_sem.at[1])
    own_far.start()

    load_table.wait()
    piece = 128

    @pl.loop(0, vectors // piece)
    def _(step):
        part = pl.ds(pl.multiple_of(step * piece, piece), piece)
        for which in range(2):
            high, low = split(table[which, part, :])
            table_high[which, part, :] = high
            table_low[which, part, :] = low

    group_rows = per_group * kpoints
    lanes = lax.broadcasted_iota(jnp.int32, (group_rows, wide), 1)
    first_half = lanes < orbitals

    @pl.loop(0, n // per_group)
    def _(group):
        for local_at in range(per_group):
            other = lax.rem(me + group * per_group + local_at, n)
            turned = inbox[other].T
            coords = [turned[:kpoints, axis : axis + 1] for axis in range(3)]

            @pl.loop(0, vectors // piece)
            def _(step):
                part = pl.ds(pl.multiple_of(step * piece, piece), piece)
                products = (
                    coords[0] * lattice[0:1, part]
                    + coords[1] * lattice[1:2, part]
                    + coords[2] * lattice[2:3, part]
                )
                cosine, sine = cos_sin(products & (KMESH - 1))
                own_rows = pl.ds(local_at * kpoints, kpoints)
                cos_high, cos_low = split(cosine)
                sin_high, sin_low = split(sine)
                waves[0, own_rows, part] = cos_high
                waves[1, own_rows, part] = cos_low
                waves[2, own_rows, part] = sin_high
                waves[3, own_rows, part] = sin_low

        block = min(256, pairs)
        for first in range(0, pairs, block):
            cols = slice(first, first + block)

            def product(wave, which):
                return (
                    dot(waves[wave], table_high[which, :, cols])
                    + dot(waves[wave], table_low[which, :, cols])
                    + dot(waves[wave + 1], table_high[which, :, cols])
                )

            real = product(0, 0) - product(2, 1)
            imag = product(0, 1) + product(2, 0)
            for pair in range(block // wide):
                span = slice(pair * wide, (pair + 1) * wide)
                real_part, imag_part = real[:, span], imag[:, span]
                even = jnp.where(first_half, real_part, pltpu.roll(imag_part, orbitals, 1))
                odd = jnp.where(first_half, pltpu.roll(real_part, orbitals, 1), imag_part)
                row = first // orbitals + 2 * pair
                for local_at in range(per_group):
                    other = lax.rem(me + group * per_group + local_at, n)
                    own = slice(local_at * kpoints, (local_at + 1) * kpoints)
                    entries_out[other, pl.ds(row, kpoints, stride=rows), :] = even[own]
                    entries_out[other, pl.ds(row + 1, kpoints, stride=rows), :] = odd[own]

    for chunk in range(len(chunks)):

        @pl.loop(1, n)
        def _(step):
            entries(step, chunk, False).start()

    own_entries = pltpu.make_async_copy(entries_out.at[me], entries_in.at[me], scalar_sem.at[2])
    own_entries.start()

    half_lane = lax.broadcasted_iota(jnp.int32, (orbitals, wide), 1) < orbitals

    @pl.loop(0, kpoints)
    def _(k):
        near = eigen[k]
        turned = pltpu.roll(near, orbitals, 1)
        lower = jnp.where(half_lane, -turned, turned)
        high, low = split(jnp.concatenate([near, lower], 0))
        near_parts[k] = jnp.concatenate([high, low], 1)

    own_far.wait()

    @pl.loop(1, n)
    def _(step):
        recv_far(step).wait_recv()

    @pl.loop(0, kpoints)
    def _(k):
        at = inbox_scalar[me, 4, k]
        far = far_in[at // capacity, lax.rem(at, capacity)]
        high = far.astype(jnp.bfloat16).astype(jnp.float32)
        far_parts[k] = jnp.concatenate([high, far - high], 0).T.astype(jnp.bfloat16)

    own_entries.wait()

    def rotate_one(k):
        matrix = entries_in[:, pl.ds(pl.multiple_of(k * rows, rows), rows), :].reshape(n * rows, wide)
        high, low = split(matrix)
        near = near_parts[k]
        right = dot(jnp.concatenate([high, low], 1), jnp.concatenate([near, near], 0))
        right = right[:, :wide] + right[:, wide:]
        right = jnp.concatenate(
            [right[mode * orbitals : (mode + 1) * orbitals] for mode in range(modes)], 1
        )
        high, low = split(right)
        far = far_parts[k]
        both = dot(jnp.concatenate([far, far], 1), jnp.concatenate([high, high, low, low], 0))
        for mode in range(modes):
            span = both[:, mode * wide : (mode + 1) * wide]
            turned = pltpu.roll(span[orbitals:], orbitals, 1)
            result[k, mode] = span[:orbitals] + jnp.where(half_lane, turned, -turned)

    def store(chunk):
        part = pl.ds(starts[chunk], chunks[chunk])
        return pltpu.make_async_copy(result.at[part], out_hbm.at[part], store_sem.at[chunk])

    for chunk in range(len(chunks)):
        together = 2 if chunks[chunk] % 2 == 0 else 1

        @pl.loop(1, n)
        def _(step):
            entries(step, chunk, True).wait_recv()

        @pl.loop(0, chunks[chunk] // together)
        def _(step):
            for extra in range(together):
                rotate_one(starts[chunk] + step * together + extra)

        store(chunk).start()

    for chunk in range(len(chunks)):
        store(chunk).wait()

        @pl.loop(1, n)
        def _(step):
            entries(step, chunk, False).wait_send()

    @pl.loop(1, n)
    def _(step):
        send_letter(step).wait_send()
        send_far(step).wait_send()


def fused(wannier_table, lattice, kpoint_grid, eigen_vectors, target_owner, target_slot):
    n = lax.axis_size("ka")
    kpoints, orbitals, wide = eigen_vectors.shape
    vectors, pairs = wannier_table.shape[1:]
    capacity = 2 * kpoints // n
    rows = pairs // orbitals
    modes = n * rows // orbitals
    per_group = math.gcd(n, 4)
    last = max(kpoints // 16, 1)
    chunks = [size for size in (kpoints - 10 * last, 6 * last, 3 * last, last) if size > 0]

    f32, bf16 = jnp.float32, jnp.bfloat16
    sizes = (n, kpoints, orbitals, vectors, pairs, capacity, per_group, chunks)
    return pl.pallas_call(
        functools.partial(kernel, sizes),
        out_shape=jax.ShapeDtypeStruct((kpoints, modes, orbitals, wide), f32),
        in_specs=[
            pl.BlockSpec(memory_space=pl.ANY),
            pl.BlockSpec(memory_space=pl.ANY),
            pl.BlockSpec(memory_space=pltpu.VMEM),
            pl.BlockSpec(memory_space=pltpu.VMEM),
            pl.BlockSpec(memory_space=pltpu.VMEM),
            pl.BlockSpec(memory_space=pltpu.VMEM),
        ],
        out_specs=pl.BlockSpec(memory_space=pl.ANY),
        scratch_shapes=[
            pltpu.VMEM((2, vectors, pairs), f32),
            pltpu.VMEM((kpoints, orbitals, wide), f32),
            pltpu.VMEM((2, vectors, pairs), bf16),
            pltpu.VMEM((2, vectors, pairs), bf16),
            pltpu.VMEM((8, 128), jnp.int32),
            pltpu.VMEM((n, 8, 128), jnp.int32),
            pltpu.SMEM((n, 8, 128), jnp.int32),
            pltpu.VMEM((n, capacity, orbitals, wide), f32),
            pltpu.VMEM((n, capacity, orbitals, wide), f32),
            pltpu.VMEM((n, kpoints * rows, wide), f32),
            pltpu.VMEM((n, kpoints * rows, wide), f32),
            pltpu.VMEM((4, per_group * kpoints, vectors), bf16),
            pltpu.VMEM((kpoints, wide, 2 * wide), bf16),
            pltpu.VMEM((kpoints, wide, wide), bf16),
            pltpu.VMEM((kpoints, modes, orbitals, wide), f32),
            pltpu.SemaphoreType.DMA((2,)),
            pltpu.SemaphoreType.DMA((3,)),
            pltpu.SemaphoreType.DMA((n,)),
            pltpu.SemaphoreType.DMA((n,)),
            pltpu.SemaphoreType.DMA((n,)),
            pltpu.SemaphoreType.DMA((n,)),
            pltpu.SemaphoreType.DMA((n, len(chunks))),
            pltpu.SemaphoreType.DMA((n, len(chunks))),
            pltpu.SemaphoreType.DMA((len(chunks),)),
        ],
        compiler_params=pltpu.CompilerParams(
            collective_id=0, has_side_effects=True, vmem_limit_bytes=60 * 1024 * 1024
        ),
    )(
        wannier_table,
        eigen_vectors,
        kpoint_grid,
        lattice,
        target_owner.reshape(1, kpoints),
        target_slot.reshape(1, kpoints),
    )


def part(wannier_table, lattice, kpoint_grid, eigen_vectors, target_owner, target_slot):
    rows = wannier_table.shape[2] // eigen_vectors.shape[1]
    tiled = (
        rows % 8 == 0
        and wannier_table.shape[1] % 128 == 0
        and eigen_vectors.shape[2] == 128
        and 2 * eigen_vectors.shape[0] <= 128
    )
    step = fused if tiled else local
    return step(wannier_table, lattice, kpoint_grid, eigen_vectors, target_owner, target_slot)


def solution(mesh):
    placed = (
        P(None, "grp", "ka"),
        P(None, "grp"),
        P(None, ("grp", "ka")),
        P(("grp", "ka"), None, None),
        P(("grp", "ka")),
        P(("grp", "ka")),
    )
    return jax.shard_map(
        part,
        mesh=mesh,
        in_specs=placed,
        out_specs=P(("grp", "ka"), None, None, None),
        check_vma=False,
    )
```
